32 devices in a mesh: fsdp: 8 (over z, x), tp: 4 (over y, core).
Axes of the slice: x: 2, y: 2, z: 4, core: 2. Of those that a mesh axis runs over, the one named last changes fastest.
Arguments:
- grad: bfloat16 [8192, 26624], P('fsdp', 'tp')
- momentum: bfloat16 [8192, 26624], P('fsdp', 'tp'), may hold values from -6 to 6
- q_prev: bfloat16 [26624, 512], P(('tp', 'fsdp')), may hold values from -6 to 6
Outputs:
- new_momentum: bfloat16 [8192, 26624], P('fsdp', 'tp')
- update: bfloat16 [8192, 26624], P('fsdp', 'tp')
- q_new: bfloat16 [26624, 512], P(('tp', 'fsdp'))
The draws below stay inside these ranges and needn't reach their ends.
All inputs are finite; a program needn't handle non-finite values.
Results may differ from the reference program's by a relative error of at most 0.009.
Values may be sent and summed in bfloat16 or wider, within the bound.
A program may use at most 192 MiB of HBM per device.

```python
import math
import jax
import jax.numpy as jnp
from jax import lax

ROWS = 8192
COLS = 26624
RANK = 512


def draw_grad(key, part):
    key = jax.random.fold_in(key, 11)
    key_base, key_rows, key_cols = jax.random.split(key, 3)
    rise_rows = 3.0 ** (jnp.arange(ROWS, dtype=jnp.float32) / ROWS)
    rise_cols = 3.0 ** (jnp.arange(COLS, dtype=jnp.float32) / COLS)
    base = jax.random.normal(key_base, (ROWS, COLS), jnp.float32)
    row_scale = jnp.exp(jax.random.uniform(key_rows, (ROWS, 1), jnp.float32) * jnp.log(10.0))
    col_scale = jnp.exp(jax.random.uniform(key_cols, (1, COLS), jnp.float32) * jnp.log(10.0))
    values = base * row_scale * col_scale * rise_rows[:, None] * rise_cols[None, :] / 30.0
    return values.astype(jnp.bfloat16)


def shard_levels(key, extent, cuts, least, high):
    gain = 1.0
    for position, shards_of in cuts:
        draws = jax.random.uniform(jax.random.fold_in(jax.random.fold_in(key, 6), position), (shards_of,), jnp.float32, least / len(cuts), high / len(cuts))
        gain = gain * jnp.repeat(jnp.exp(draws), extent[position] // shards_of).reshape((-1,) + (1,) * (len(extent) - 1 - position))
    return gain


def bell_draw(stream_key, dims, width, bound, cuts=(), kind=jnp.bfloat16):
    drawn = jax.random.normal(stream_key, dims, jnp.float32) * width
    if len(cuts) > 0:
        drawn = shard_levels(stream_key, dims, cuts, -0.22, 0.18) * drawn
    return jnp.clip(drawn, min=-bound, max=bound).astype(kind)


def setup_inputs(seed: int = 0) -> dict:
    splits = jax.random.split(jax.random.key(seed), 4)
    grad = draw_grad(jax.random.fold_in(splits[3], 71), 0)
    momentum = bell_draw(splits[1], (ROWS, COLS), 1.0, 6.0, ((0, 8), (1, 4)))
    q_prev = bell_draw(splits[2], (COLS, RANK), 1.0, 6.0, ((0, 32),))
    return dict(grad=grad, momentum=momentum, q_prev=q_prev)


def contract_rows(left, right, precision=None):
    return lax.dot_general(left.astype(jnp.float32), right.astype(jnp.float32), (((0,), (0,)), ((), ())), precision=precision, preferred_element_type=jnp.float32)

def contract_cols(left, right):
    return lax.dot_general(left.astype(jnp.float32), right.astype(jnp.float32), (((1,), (1,)), ((), ())), preferred_element_type=jnp.float32)

def reference(grad, momentum, q_prev):
    blended = (momentum.astype(jnp.float32) + grad.astype(jnp.float32)).astype(jnp.bfloat16)
    projected = jnp.dot(blended.astype(jnp.float32), q_prev.astype(jnp.float32), preferred_element_type=jnp.float32)
    gram_matrix = contract_rows(projected, projected, lax.Precision.HIGHEST)
    cholesky_factor = jnp.linalg.cholesky(gram_matrix)
    orthonormal = lax.linalg.triangular_solve(cholesky_factor, projected, left_side=False, lower=True, transpose_a=True)
    ortho_low = orthonormal.astype(jnp.bfloat16)
    reduced = contract_rows(blended, ortho_low)
    col_norms = jnp.sqrt(lax.optimization_barrier(jnp.sum(reduced * reduced, axis=0))) + 1e-06
    q_new = (math.sqrt(COLS) * reduced / col_norms).astype(jnp.bfloat16)
    weighted = (orthonormal * col_norms / math.sqrt(COLS)).astype(jnp.bfloat16)
    new_momentum = (blended.astype(jnp.float32) - 0.05 * contract_cols(weighted, q_new)).astype(jnp.bfloat16)
    update = (math.sqrt(ROWS / RANK) * contract_cols(ortho_low, q_new)).astype(jnp.bfloat16)
    return (new_momentum, update, q_new)
```

```python
import functools
import math

import jax
import jax.numpy as jnp
from jax import lax
from jax.experimental import pallas as pl
from jax.experimental.pallas import tpu as pltpu
from jax.sharding import PartitionSpec as P

MESH = pl.DeviceIdType.MESH
MIB = 1024 * 1024


def contract_rows(left, right, precision=None):
    return lax.dot_general(
        left,
        right,
        (((0,), (0,)), ((), ())),
        precision=precision,
        preferred_element_type=jnp.float32,
    )


def contract_cols(left, right):
    return lax.dot_general(
        left, right, (((1,), (1,)), ((), ())), preferred_element_type=jnp.float32
    )


def orthonormalize(gram_matrix, projected):
    cholesky_factor = jnp.linalg.cholesky(gram_matrix)
    return lax.linalg.triangular_solve(
        cholesky_factor, projected, left_side=False, lower=True, transpose_a=True
    )


def ring_place(index, n):
    pair = lax.div(index, 2)
    return pair + lax.rem(index, 2) * (n - 1 - 2 * pair)


def ring_index(place, n):
    place = lax.rem(place + 2 * n, n)
    upper = lax.div(place, n // 2)
    return 2 * place + upper * (2 * n - 1 - 4 * place)


def piece_of(rows):
    return max(p for p in range(16, 209, 16) if rows % p == 0)


def greet(devices):
    barrier = pltpu.get_barrier_semaphore()
    for device in devices:
        pl.semaphore_signal(barrier, inc=1, device_id=device, device_id_type=MESH)
    pl.semaphore_wait(barrier, len(devices))


def gather_steps(n, place, own_ref, out_ref, send_sem, recv_sem, on_block=None):
    half = n // 2
    width = out_ref.shape[2] // 2
    targets = (ring_index(place + 1, n), ring_index(place - 1, n))
    copies = {}
    for step in range(half):
        for chunk in (0, 1):
            for way in (0, 1):
                if step == half - 1 and chunk != way:
                    continue
                owner = ring_index(place - step if way == 0 else place + step, n)
                lanes = pl.ds(chunk * width, width)
                if step > 0:
                    copies[way, step - 1, chunk].wait_recv()
                source = own_ref if step == 0 else out_ref.at[owner]
                copy = pltpu.make_async_remote_copy(
                    src_ref=source.at[:, lanes],
                    dst_ref=out_ref.at[owner, :, lanes],
                    send_sem=send_sem.at[way, step, chunk],
                    recv_sem=recv_sem.at[way, step, chunk],
                    device_id={"fsdp": targets[way]},
                    device_id_type=MESH,
                )
                copy.start()
                copies[way, step, chunk] = copy
                if on_block is not None and (step > 0 or way == 0):
                    on_block(owner, chunk)
    for way in (0, 1):
        copies[way, half - 2, 1 - way].wait_recv()
        if on_block is not None:
            owner = ring_index(place - half + 1 if way == 0 else place + half - 1, n)
            on_block(owner, 1 - way)
    for way in (0, 1):
        copies[way, half - 1, way].wait_recv()
        if on_block is not None:
            on_block(ring_index(place + half, n), way)
    for copy in copies.values():
        copy.wait_send()


def gather_kernel(n, own_ref, out_ref, local_sem, send_sem, recv_sem):
    me = lax.axis_index("fsdp")
    place = ring_place(me, n)
    greet([{"fsdp": ring_index(place + 1, n)}, {"fsdp": ring_index(place - 1, n)}])
    local = pltpu.make_async_copy(own_ref, out_ref.at[me], local_sem)
    local.start()
    gather_steps(n, place, own_ref, out_ref, send_sem, recv_sem)
    local.wait()


def gather_rows(rows):
    n = lax.axis_size("fsdp")
    return pl.pallas_call(
        functools.partial(gather_kernel, n),
        out_shape=jax.ShapeDtypeStruct((n,) + rows.shape, rows.dtype),
        in_specs=[pl.BlockSpec(memory_space=pl.ANY)],
        out_specs=pl.BlockSpec(memory_space=pl.ANY),
        scratch_shapes=[
            pltpu.SemaphoreType.DMA(()),
            pltpu.SemaphoreType.DMA((2, n // 2, 2)),
            pltpu.SemaphoreType.DMA((2, n // 2, 2)),
        ],
        compiler_params=pltpu.CompilerParams(collective_id=0, has_side_effects=True),
        name="gather_rows",
    )(rows)


def sum_gather_kernel(
    n,
    tps,
    part_ref,
    all_ref,
    own_ref,
    squares_ref,
    land,
    acc,
    others,
    sum_send,
    sum_recv,
    send_sem,
    recv_sem,
    sq_send,
    sq_recv,
):
    half = n // 2
    me = lax.axis_index("fsdp")
    col = lax.axis_index("tp")
    place = ring_place(me, n)
    rows, cols = part_ref.shape[1:]
    width = cols // 2
    piece = piece_of(rows)
    targets = (ring_index(place + 1, n), ring_index(place - 1, n))
    peers = [lax.rem(col + d, tps) for d in range(1, tps)]
    greet([{"fsdp": t} for t in targets] + [{"tp": p} for p in peers])

    copies = {}
    for step in range(half):
        for chunk in (0, 1):
            for way in (0, 1):
                if step == 0 and chunk != way:
                    continue
                lanes = pl.ds(chunk * width, width)
                away = half - step
                owner = ring_index(place + away if way == 0 else place - away, n)
                if step == 0 or (step == 1 and chunk != way):
                    source = part_ref.at[owner, :, lanes]
                else:
                    copies[way, step - 1, chunk].wait_recv()

                    @pl.loop(0, rows // piece)
                    def _(i, way=way, step=step, lanes=lanes, owner=owner):
                        at = pl.ds(pl.multiple_of(i * piece, 16), piece)
                        land[way, step - 1, at, lanes] = (
                            land[way, step - 1, at, lanes].astype(jnp.float32)
                            + part_ref[owner, at, lanes].astype(jnp.float32)
                        ).astype(jnp.bfloat16)

                    source = land.at[way, step - 1, :, lanes]
                copy = pltpu.make_async_remote_copy(
                    src_ref=source,
                    dst_ref=land.at[way, step, :, lanes],
                    send_sem=sum_send.at[way, step, chunk],
                    recv_sem=sum_recv.at[way, step, chunk],
                    device_id={"fsdp": targets[way]},
                    device_id_type=MESH,
                )
                copy.start()
                copies[way, step, chunk] = copy

    for chunk in (0, 1):
        lanes = pl.ds(chunk * width, width)
        for way in (0, 1):
            copies[way, half - 1, chunk].wait_recv()

        @pl.loop(0, rows // piece)
        def _(i, lanes=lanes):
            at = pl.ds(pl.multiple_of(i * piece, 16), piece)
            total = (
                part_ref[me, at, lanes].astype(jnp.float32)
                + land[0, half - 1, at, lanes].astype(jnp.float32)
                + land[1, half - 1, at, lanes].astype(jnp.float32)
            )
            own_ref[at, lanes] = total
            all_ref[me, at, lanes] = total.astype(jnp.bfloat16)

    acc[...] = jnp.zeros_like(acc)

    def on_block(owner, chunk):
        lanes = pl.ds(chunk * width, width)

        @pl.loop(0, rows // piece)
        def _(i):
            at = pl.ds(pl.multiple_of(i * piece, 16), piece)
            block = all_ref[owner, at, lanes].astype(jnp.float32)
            acc[:, lanes] += jnp.sum((block * block).reshape(piece // 8, 8, width), axis=0)

    gather_steps(n, place, all_ref.at[me], all_ref, send_sem, recv_sem, on_block)

    sends = []
    for d, peer in enumerate(peers):
        copy = pltpu.make_async_remote_copy(
            src_ref=acc,
            dst_ref=others.at[d],
            send_sem=sq_send.at[d],
            recv_sem=sq_recv.at[d],
            device_id={"tp": peer},
            device_id_type=MESH,
        )
        copy.start()
        sends.append(copy)
    for copy in copies.values():
        copy.wait_send()
    total = acc[...]
    for d, copy in enumerate(sends):
        copy.wait_recv()
        total = total + others[d]
    squares_ref[...] = jnp.sum(total, axis=0, keepdims=True)
    for copy in sends:
        copy.wait_send()


def sum_and_gather(parts):
    n, rows, cols = parts.shape
    half = n // 2
    tps = lax.axis_size("tp")
    vmem = pl.BlockSpec(memory_space=pltpu.VMEM)
    return pl.pallas_call(
        functools.partial(sum_gather_kernel, n, tps),
        out_shape=(
            jax.ShapeDtypeStruct((n, rows, cols), jnp.bfloat16),
            jax.ShapeDtypeStruct((rows, cols), jnp.float32),
            jax.ShapeDtypeStruct((1, cols), jnp.float32),
        ),
        in_specs=[vmem],
        out_specs=(vmem, vmem, vmem),
        scratch_shapes=[
            pltpu.VMEM((2, half, rows, cols), jnp.bfloat16),
            pltpu.VMEM((8, cols), jnp.float32),
            pltpu.VMEM((tps - 1, 8, cols), jnp.float32),
            pltpu.SemaphoreType.DMA((2, half, 2)),
            pltpu.SemaphoreType.DMA((2, half, 2)),
            pltpu.SemaphoreType.DMA((2, half, 2)),
            pltpu.SemaphoreType.DMA((2, half, 2)),
            pltpu.SemaphoreType.DMA((tps - 1,)),
            pltpu.SemaphoreType.DMA((tps - 1,)),
        ],
        compiler_params=pltpu.CompilerParams(
            collective_id=1, has_side_effects=True, vmem_limit_bytes=48 * MIB
        ),
        name="sum_and_gather",
    )(parts)


def per_device(grad, momentum, q_prev):
    blended = (momentum.astype(jnp.float32) + grad.astype(jnp.float32)).astype(jnp.bfloat16)
    rows_dev, cols_dev = blended.shape
    part_rows, width = q_prev.shape
    shards = lax.axis_size("fsdp")
    cols_total = cols_dev * lax.axis_size("tp")
    rows_total = rows_dev * shards
    basis = gather_rows(q_prev).reshape(cols_dev, width)
    partial_proj = jnp.dot(blended, basis, preferred_element_type=jnp.float32)
    projected = lax.psum(partial_proj, "tp")
    local_gram = contract_rows(projected, projected, lax.Precision.HIGHEST)
    gram_matrix = lax.psum(local_gram, "fsdp")
    orthonormal = orthonormalize(gram_matrix, projected)
    ortho_low = orthonormal.astype(jnp.bfloat16)
    update_scale = math.sqrt(rows_total / width)
    parts = contract_rows(blended, ortho_low).astype(jnp.bfloat16)
    gathered, reduced, squares = sum_and_gather(parts.reshape(shards, part_rows, width))
    inverse = math.sqrt(cols_total) / (jnp.sqrt(squares) + 1e-06)
    q_new = (reduced * inverse).astype(jnp.bfloat16)
    steer_left = (orthonormal * (update_scale * inverse)).astype(jnp.bfloat16)
    gathered = gathered.reshape(cols_dev, width)
    new_momentum = (
        blended.astype(jnp.float32) - 0.05 * contract_cols(ortho_low, gathered)
    ).astype(jnp.bfloat16)
    update = contract_cols(steer_left, gathered).astype(jnp.bfloat16)
    return (new_momentum, update, q_new)


def solution(mesh):
    return jax.shard_map(
        per_device,
        mesh=mesh,
        in_specs=(P("fsdp", "tp"), P("fsdp", "tp"), P(("tp", "fsdp"), None)),
        out_specs=(P("fsdp", "tp"), P("fsdp", "tp"), P(("tp", "fsdp"), None)),
        check_vma=False,
    )
```

```python
import functools
import math

import jax
import jax.numpy as jnp
from jax import lax
from jax.experimental import pallas as pl
from jax.experimental.pallas import tpu as pltpu
from jax.sharding import PartitionSpec as P

MESH = pl.DeviceIdType.MESH
MIB = 1024 * 1024


def contract_rows(left, right, precision=None):
    return lax.dot_general(
        left,
        right,
        (((0,), (0,)), ((), ())),
        precision=precision,
        preferred_element_type=jnp.float32,
    )


def contract_cols(left, right):
    return lax.dot_general(
        left, right, (((1,), (1,)), ((), ())), preferred_element_type=jnp.float32
    )


def factor_inverse(block):
    size = block.shape[0]
    group = 8
    row = lax.broadcasted_iota(jnp.int32, (size, 1), 0)
    eye = (
        lax.broadcasted_iota(jnp.int32, (size, size), 0)
        == lax.broadcasted_iota(jnp.int32, (size, size), 1)
    )

    def eliminate(step, carry):
        left, right = carry
        for s in range(group):
            pivot = left[s : s + 1, s : s + 1]
            active = (row > s) & (row < size - group * step)
            scale = jnp.where(active, left[:, s : s + 1] * (1.0 / pivot), 0.0)
            left = left - scale * left[s : s + 1, :]
            right = right - scale * right[s : s + 1, :]
        left = pltpu.roll(jnp.concatenate([left[group:], left[:group]], axis=0), size - group, 1)
        right = jnp.concatenate([right[group:], right[:group]], axis=0)
        return left, right

    left, right = lax.fori_loop(
        0, size // group, eliminate, (block, jnp.where(eye, 1.0, 0.0).astype(jnp.float32))
    )
    diagonal = jnp.sum(jnp.where(eye, left, 0.0), axis=1, keepdims=True)
    return right / jnp.sqrt(diagonal)


def orthonormalize_kernel(block, gram_ref, proj_ref, ortho_ref, gram, proj):
    size = gram_ref.shape[0]
    gram[...] = gram_ref[...]
    proj[...] = proj_ref[...]

    def times_transposed(left, right):
        return lax.dot_general(
            left,
            right,
            (((1,), (1,)), ((), ())),
            precision=lax.Precision.HIGHEST,
            preferred_element_type=jnp.float32,
        )

    for start in range(0, size, block):
        end = start + block
        inverse = factor_inverse(gram[start:end, start:end])
        solved = times_transposed(proj[:, start:end], inverse)
        ortho_ref[:, start:end] = solved
        if end < size:
            panel = times_transposed(gram[end:, start:end], inverse)
            gram[end:, end:] -= times_transposed(panel, panel)
            proj[:, end:] -= times_transposed(solved, panel)


def orthonormalize(gram_matrix, projected):
    vmem = pl.BlockSpec(memory_space=pltpu.VMEM)
    return pl.pallas_call(
        functools.partial(orthonormalize_kernel, 128),
        out_shape=jax.ShapeDtypeStruct(projected.shape, jnp.float32),
        in_specs=[vmem, vmem],
        out_specs=vmem,
        scratch_shapes=[
            pltpu.VMEM(gram_matrix.shape, jnp.float32),
            pltpu.VMEM(projected.shape, jnp.float32),
        ],
        compiler_params=pltpu.CompilerParams(vmem_limit_bytes=40 * MIB),
        name="orthonormalize",
    )(gram_matrix, projected)


def ring_place(index, n):
    pair = lax.div(index, 2)
    return pair + lax.rem(index, 2) * (n - 1 - 2 * pair)


def ring_index(place, n):
    place = lax.rem(place + 2 * n, n)
    upper = lax.div(place, n // 2)
    return 2 * place + upper * (2 * n - 1 - 4 * place)


def piece_of(rows):
    return max(p for p in range(16, 209, 16) if rows % p == 0)


def greet(devices):
    barrier = pltpu.get_barrier_semaphore()
    for device in devices:
        pl.semaphore_signal(barrier, inc=1, device_id=device, device_id_type=MESH)
    pl.semaphore_wait(barrier, len(devices))


def gather_steps(n, place, own_ref, out_ref, send_sem, recv_sem, on_block=None):
    half = n // 2
    width = out_ref.shape[2] // 2
    targets = (ring_index(place + 1, n), ring_index(place - 1, n))
    copies = {}
    for step in range(half):
        for chunk in (0, 1):
            for way in (0, 1):
                if step == half - 1 and chunk != way:
                    continue
                owner = ring_index(place - step if way == 0 else place + step, n)
                lanes = pl.ds(chunk * width, width)
                if step > 0:
                    copies[way, step - 1, chunk].wait_recv()
                source = own_ref if step == 0 else out_ref.at[owner]
                copy = pltpu.make_async_remote_copy(
                    src_ref=source.at[:, lanes],
                    dst_ref=out_ref.at[owner, :, lanes],
                    send_sem=send_sem.at[way, step, chunk],
                    recv_sem=recv_sem.at[way, step, chunk],
                    device_id={"fsdp": targets[way]},
                    device_id_type=MESH,
                )
                copy.start()
                copies[way, step, chunk] = copy
                if on_block is not None and (step > 0 or way == 0):
                    on_block(owner, chunk)
    for way in (0, 1):
        copies[way, half - 2, 1 - way].wait_recv()
        if on_block is not None:
            owner = ring_index(place - half + 1 if way == 0 else place + half - 1, n)
            on_block(owner, 1 - way)
    for way in (0, 1):
        copies[way, half - 1, way].wait_recv()
        if on_block is not None:
            on_block(ring_index(place + half, n), way)
    for copy in copies.values():
        copy.wait_send()


def gather_kernel(n, own_ref, out_ref, local_sem, send_sem, recv_sem):
    me = lax.axis_index("fsdp")
    place = ring_place(me, n)
    greet([{"fsdp": ring_index(place + 1, n)}, {"fsdp": ring_index(place - 1, n)}])
    local = pltpu.make_async_copy(own_ref, out_ref.at[me], local_sem)
    local.start()
    gather_steps(n, place, own_ref, out_ref, send_sem, recv_sem)
    local.wait()


def gather_rows(rows):
    n = lax.axis_size("fsdp")
    return pl.pallas_call(
        functools.partial(gather_kernel, n),
        out_shape=jax.ShapeDtypeStruct((n,) + rows.shape, rows.dtype),
        in_specs=[pl.BlockSpec(memory_space=pl.ANY)],
        out_specs=pl.BlockSpec(memory_space=pl.ANY),
        scratch_shapes=[
            pltpu.SemaphoreType.DMA(()),
            pltpu.SemaphoreType.DMA((2, n // 2, 2)),
            pltpu.SemaphoreType.DMA((2, n // 2, 2)),
        ],
        compiler_params=pltpu.CompilerParams(collective_id=0, has_side_effects=True),
        name="gather_rows",
    )(rows)


def sum_gather_kernel(
    n,
    tps,
    part_ref,
    all_ref,
    own_ref,
    squares_ref,
    land,
    acc,
    others,
    sum_send,
    sum_recv,
    send_sem,
    recv_sem,
    sq_send,
    sq_recv,
):
    half = n // 2
    me = lax.axis_index("fsdp")
    col = lax.axis_index("tp")
    place = ring_place(me, n)
    rows, cols = part_ref.shape[1:]
    width = cols // 2
    piece = piece_of(rows)
    targets = (ring_index(place + 1, n), ring_index(place - 1, n))
    peers = [lax.rem(col + d, tps) for d in range(1, tps)]
    greet([{"fsdp": t} for t in targets] + [{"tp": p} for p in peers])

    copies = {}
    for step in range(half):
        for chunk in (0, 1):
            for way in (0, 1):
                if step == 0 and chunk != way:
                    continue
                lanes = pl.ds(chunk * width, width)
                away = half - step
                owner = ring_index(place + away if way == 0 else place - away, n)
                if step == 0 or (step == 1 and chunk != way):
                    source = part_ref.at[owner, :, lanes]
                else:
                    copies[way, step - 1, chunk].wait_recv()

                    @pl.loop(0, rows // piece)
                    def _(i, way=way, step=step, lanes=lanes, owner=owner):
                        at = pl.ds(pl.multiple_of(i * piece, 16), piece)
                        land[way, step - 1, at, lanes] = (
                            land[way, step - 1, at, lanes].astype(jnp.float32)
                            + part_ref[owner, at, lanes].astype(jnp.float32)
                        ).astype(jnp.bfloat16)

                    source = land.at[way, step - 1, :, lanes]
                copy = pltpu.make_async_remote_copy(
                    src_ref=source,
                    dst_ref=land.at[way, step, :, lanes],
                    send_sem=sum_send.at[way, step, chunk],
                    recv_sem=sum_recv.at[way, step, chunk],
                    device_id={"fsdp": targets[way]},
                    device_id_type=MESH,
                )
                copy.start()
                copies[way, step, chunk] = copy

    for chunk in (0, 1):
        lanes = pl.ds(chunk * width, width)
        for way in (0, 1):
            copies[way, half - 1, chunk].wait_recv()

        @pl.loop(0, rows // piece)
        def _(i, lanes=lanes):
            at = pl.ds(pl.multiple_of(i * piece, 16), piece)
            total = (
                part_ref[me, at, lanes].astype(jnp.float32)
                + land[0, half - 1, at, lanes].astype(jnp.float32)
                + land[1, half - 1, at, lanes].astype(jnp.float32)
            )
            own_ref[at, lanes] = total
            all_ref[me, at, lanes] = total.astype(jnp.bfloat16)

    acc[...] = jnp.zeros_like(acc)

    def on_block(owner, chunk):
        lanes = pl.ds(chunk * width, width)

        @pl.loop(0, rows // piece)
        def _(i):
            at = pl.ds(pl.multiple_of(i * piece, 16), piece)
            block = all_ref[owner, at, lanes].astype(jnp.float32)
            acc[:, lanes] += jnp.sum((block * block).reshape(piece // 8, 8, width), axis=0)

    gather_steps(n, place, all_ref.at[me], all_ref, send_sem, recv_sem, on_block)

    sends = []
    for d, peer in enumerate(peers):
        copy = pltpu.make_async_remote_copy(
            src_ref=acc,
            dst_ref=others.at[d],
            send_sem=sq_send.at[d],
            recv_sem=sq_recv.at[d],
            device_id={"tp": peer},
            device_id_type=MESH,
        )
        copy.start()
        sends.append(copy)
    for copy in copies.values():
        copy.wait_send()
    total = acc[...]
    for d, copy in enumerate(sends):
        copy.wait_recv()
        total = total + others[d]
    squares_ref[...] = jnp.sum(total, axis=0, keepdims=True)
    for copy in sends:
        copy.wait_send()


def sum_and_gather(parts):
    n, rows, cols = parts.shape
    half = n // 2
    tps = lax.axis_size("tp")
    vmem = pl.BlockSpec(memory_space=pltpu.VMEM)
    return pl.pallas_call(
        functools.partial(sum_gather_kernel, n, tps),
        out_shape=(
            jax.ShapeDtypeStruct((n, rows, cols), jnp.bfloat16),
            jax.ShapeDtypeStruct((rows, cols), jnp.float32),
            jax.ShapeDtypeStruct((1, cols), jnp.float32),
        ),
        in_specs=[vmem],
        out_specs=(vmem, vmem, vmem),
        scratch_shapes=[
            pltpu.VMEM((2, half, rows, cols), jnp.bfloat16),
            pltpu.VMEM((8, cols), jnp.float32),
            pltpu.VMEM((tps - 1, 8, cols), jnp.float32),
            pltpu.SemaphoreType.DMA((2, half, 2)),
            pltpu.SemaphoreType.DMA((2, half, 2)),
            pltpu.SemaphoreType.DMA((2, half, 2)),
            pltpu.SemaphoreType.DMA((2, half, 2)),
            pltpu.SemaphoreType.DMA((tps - 1,)),
            pltpu.SemaphoreType.DMA((tps - 1,)),
        ],
        compiler_params=pltpu.CompilerParams(
            collective_id=1, has_side_effects=True, vmem_limit_bytes=48 * MIB
        ),
        name="sum_and_gather",
    )(parts)


def partner(index, bit):
    return index + bit - 2 * bit * lax.rem(lax.div(index, bit), 2)


def bits_below(count):
    return [1 << k for k in range(count.bit_length() - 1)]


def project_gram_kernel(n, tps, part_ref, proj_ref, gram_ref, sums, land, halves, terms, send, recv):
    col = lax.axis_index("tp")
    row = lax.axis_index("fsdp")
    tp_bits, row_bits = bits_below(tps), bits_below(n)
    greet(
        [{"tp": partner(col, b)} for b in tp_bits] + [{"fsdp": partner(row, b)} for b in row_bits]
    )
    used = []

    def exchange(source, target, device):
        k = len(used)
        copy = pltpu.make_async_remote_copy(
            src_ref=source,
            dst_ref=target,
            send_sem=send.at[k],
            recv_sem=recv.at[k],
            device_id=device,
            device_id_type=MESH,
        )
        copy.start()
        used.append(copy)
        copy.wait_recv()

    rows, cols = part_ref.shape
    source, extent, base, top = part_ref, rows, 0, 0
    for k, bit in enumerate(tp_bits):
        extent //= 2
        high = lax.rem(lax.div(col, bit), 2)
        keep = pl.ds(pl.multiple_of(high * extent, 8), extent)
        give = pl.ds(pl.multiple_of((1 - high) * extent, 8), extent)
        exchange(source.at[give], land.at[pl.ds(top, extent)], {"tp": partner(col, bit)})
        base = base + high * extent
        arrived = land[pl.ds(top, extent)]
        if k == len(tp_bits) - 1:
            proj_ref[pl.ds(pl.multiple_of(base, 8), extent)] = source[keep] + arrived
        else:
            sums[pl.ds(top, extent)] = source[keep] + arrived
            source = sums.at[pl.ds(top, extent)]
        top += extent

    def spread(ref, extent):
        for bit in reversed(tp_bits):
            start = 0
            for k, other in enumerate(tp_bits):
                if other < bit or other == bit:
                    start = start + lax.rem(lax.div(col, other), 2) * (ref.shape[0] >> (k + 1))
            held = pl.ds(pl.multiple_of(start, 8), extent)
            exchange(ref.at[held], ref.at[held], {"tp": partner(col, bit)})
            extent *= 2

    spread(proj_ref, extent)

    strip = cols // tps
    first = 0
    for k, bit in enumerate(tp_bits):
        first = first + lax.rem(lax.div(col, bit), 2) * (cols >> (k + 1))
    own = pl.ds(pl.multiple_of(first, strip), strip)
    halves[0] = lax.dot_general(
        proj_ref[:, own],
        proj_ref[...],
        (((0,), (0,)), ((), ())),
        precision=lax.Precision.HIGHEST,
        preferred_element_type=jnp.float32,
    )
    for k, bit in enumerate(row_bits):
        exchange(halves.at[k], terms.at[k], {"fsdp": partner(row, bit)})
        total = halves[k] + terms[k]
        if k == len(row_bits) - 1:
            gram_ref[own] = total
        else:
            halves[k + 1] = total
    spread(gram_ref, strip)
    for copy in used:
        copy.wait_send()


def project_gram(partial_proj):
    rows, cols = partial_proj.shape
    n, tps = lax.axis_size("fsdp"), lax.axis_size("tp")
    stages = 2 * len(bits_below(tps)) + len(bits_below(n)) + len(bits_below(tps))
    levels = len(bits_below(n))
    vmem = pl.BlockSpec(memory_space=pltpu.VMEM)
    return pl.pallas_call(
        functools.partial(project_gram_kernel, n, tps),
        out_shape=(
            jax.ShapeDtypeStruct((rows, cols), jnp.float32),
            jax.ShapeDtypeStruct((cols, cols), jnp.float32),
        ),
        in_specs=[vmem],
        out_specs=(vmem, vmem),
        scratch_shapes=[
            pltpu.VMEM((rows, cols), jnp.float32),
            pltpu.VMEM((rows, cols), jnp.float32),
            pltpu.VMEM((levels, cols // tps, cols), jnp.float32),
            pltpu.VMEM((levels, cols // tps, cols), jnp.float32),
            pltpu.SemaphoreType.DMA((stages,)),
            pltpu.SemaphoreType.DMA((stages,)),
        ],
        compiler_params=pltpu.CompilerParams(
            collective_id=2, has_side_effects=True, vmem_limit_bytes=40 * MIB
        ),
        name="project_gram",
    )(partial_proj)


def per_device(grad, momentum, q_prev):
    blended = (momentum.astype(jnp.float32) + grad.astype(jnp.float32)).astype(jnp.bfloat16)
    rows_dev, cols_dev = blended.shape
    part_rows, width = q_prev.shape
    shards = lax.axis_size("fsdp")
    cols_total = cols_dev * lax.axis_size("tp")
    rows_total = rows_dev * shards
    basis = gather_rows(q_prev).reshape(cols_dev, width)
    partial_proj = jnp.dot(blended, basis, preferred_element_type=jnp.float32)
    projected, gram_matrix = project_gram(partial_proj)
    orthonormal = orthonormalize(gram_matrix, projected)
    ortho_low = orthonormal.astype(jnp.bfloat16)
    update_scale = math.sqrt(rows_total / width)
    parts = contract_rows(blended, ortho_low).astype(jnp.bfloat16)
    gathered, reduced, squares = sum_and_gather(parts.reshape(shards, part_rows, width))
    inverse = math.sqrt(cols_total) / (jnp.sqrt(squares) + 1e-06)
    q_new = (reduced * inverse).astype(jnp.bfloat16)
    steer_left = (orthonormal * (update_scale * inverse)).astype(jnp.bfloat16)
    gathered = gathered.reshape(cols_dev, width)
    new_momentum = (
        blended.astype(jnp.float32) - 0.05 * contract_cols(ortho_low, gathered)
    ).astype(jnp.bfloat16)
    update = contract_cols(steer_left, gathered).astype(jnp.bfloat16)
    return (new_momentum, update, q_new)


def solution(mesh):
    return jax.shard_map(
        per_device,
        mesh=mesh,
        in_specs=(P("fsdp", "tp"), P("fsdp", "tp"), P(("tp", "fsdp"), None)),
        out_specs=(P("fsdp", "tp"), P("fsdp", "tp"), P(("tp", "fsdp"), None)),
        check_vma=False,
    )
```

```python
import functools
import math

import jax
import jax.numpy as jnp
from jax import lax
from jax.experimental import pallas as pl
from jax.experimental.pallas import tpu as pltpu
from jax.sharding import PartitionSpec as P

MESH = pl.DeviceIdType.MESH
MIB = 1024 * 1024


def contract_rows(left, right, precision=None):
    return lax.dot_general(
        left,
        right,
        (((0,), (0,)), ((), ())),
        precision=precision,
        preferred_element_type=jnp.float32,
    )


def contract_cols(left, right):
    return lax.dot_general(
        left, right, (((1,), (1,)), ((), ())), preferred_element_type=jnp.float32
    )


def factor_inverse(block):
    size = block.shape[0]
    group = 16
    row = lax.broadcasted_iota(jnp.int32, (size, 1), 0)
    eye = (
        lax.broadcasted_iota(jnp.int32, (size, size), 0)
        == lax.broadcasted_iota(jnp.int32, (size, size), 1)
    )

    def eliminate(step, carry):
        left, right = carry
        for s in range(group):
            active = (row > s) & (row < size - group * step)
            column = jnp.broadcast_to(left[:, s : s + 1], left.shape)
            inverse = 1.0 / column[s : s + 1, :]
            column = jnp.where(active, column, 0.0)
            left, right = (
                left - column * (left[s : s + 1, :] * inverse),
                right - column * (right[s : s + 1, :] * inverse),
            )
        left = pltpu.roll(jnp.concatenate([left[group:], left[:group]], axis=0), size - group, 1)
        right = jnp.concatenate([right[group:], right[:group]], axis=0)
        return left, right

    left, right = lax.fori_loop(
        0, size // group, eliminate, (block, jnp.where(eye, 1.0, 0.0).astype(jnp.float32))
    )
    diagonal = jnp.sum(jnp.where(eye, left, 0.0), axis=1, keepdims=True)
    return right / jnp.sqrt(diagonal)


def orthonormalize_kernel(block, gram_ref, proj_ref, ortho_ref, gram, proj):
    size = gram_ref.shape[0]
    gram[...] = gram_ref[...]
    proj[...] = proj_ref[...]

    def times_transposed(left, right):
        return lax.dot_general(
            left,
            right,
            (((1,), (1,)), ((), ())),
            precision=lax.Precision.HIGHEST,
            preferred_element_type=jnp.float32,
        )

    for start in range(0, size, block):
        end = start + block
        inverse = factor_inverse(gram[start:end, start:end])
        solved = times_transposed(proj[:, start:end], inverse)
        ortho_ref[:, start:end] = solved
        if end < size:
            panel = times_transposed(gram[end:, start:end], inverse)
            gram[end:, end:] -= times_transposed(panel, panel)
            proj[:, end:] -= times_transposed(solved, panel)


def orthonormalize(gram_matrix, projected):
    vmem = pl.BlockSpec(memory_space=pltpu.VMEM)
    return pl.pallas_call(
        functools.partial(orthonormalize_kernel, 128),
        out_shape=jax.ShapeDtypeStruct(projected.shape, jnp.float32),
        in_specs=[vmem, vmem],
        out_specs=vmem,
        scratch_shapes=[
            pltpu.VMEM(gram_matrix.shape, jnp.float32),
            pltpu.VMEM(projected.shape, jnp.float32),
        ],
        compiler_params=pltpu.CompilerParams(vmem_limit_bytes=40 * MIB),
        name="orthonormalize",
    )(gram_matrix, projected)


def ring_place(index, n):
    pair = lax.div(index, 2)
    return pair + lax.rem(index, 2) * (n - 1 - 2 * pair)


def ring_index(place, n):
    place = lax.rem(place + 2 * n, n)
    upper = lax.div(place, n // 2)
    return 2 * place + upper * (2 * n - 1 - 4 * place)


def piece_of(rows):
    return max(p for p in range(16, 209, 16) if rows % p == 0)


def greet(devices):
    barrier = pltpu.get_barrier_semaphore()
    for device in devices:
        pl.semaphore_signal(barrier, inc=1, device_id=device, device_id_type=MESH)
    pl.semaphore_wait(barrier, len(devices))


def gather_steps(n, place, own_ref, out_ref, send_sem, recv_sem, on_block=None, on_step=None):
    half = n // 2
    width = out_ref.shape[2] // 2
    targets = (ring_index(place + 1, n), ring_index(place - 1, n))
    copies = {}
    for step in range(half):
        for chunk in (0, 1):
            for way in (0, 1):
                if step == half - 1 and chunk != way:
                    continue
                owner = ring_index(place - step if way == 0 else place + step, n)
                lanes = pl.ds(chunk * width, width)
                if step > 0:
                    copies[way, step - 1, chunk].wait_recv()
                source = own_ref if step == 0 else out_ref.at[owner]
                copy = pltpu.make_async_remote_copy(
                    src_ref=source.at[:, lanes],
                    dst_ref=out_ref.at[owner, :, lanes],
                    send_sem=send_sem.at[way, step, chunk],
                    recv_sem=recv_sem.at[way, step, chunk],
                    device_id={"fsdp": targets[way]},
                    device_id_type=MESH,
                )
                copy.start()
                copies[way, step, chunk] = copy
                if on_block is not None and (step > 0 or way == 0):
                    on_block(owner, chunk)
        if on_step is not None:
            on_step(step)
    for way in (0, 1):
        copies[way, half - 2, 1 - way].wait_recv()
        if on_block is not None:
            owner = ring_index(place - half + 1 if way == 0 else place + half - 1, n)
            on_block(owner, 1 - way)
    for way in (0, 1):
        copies[way, half - 1, way].wait_recv()
        if on_block is not None:
            on_block(ring_index(place + half, n), way)
    for copy in copies.values():
        copy.wait_send()


def blend_gather_kernel(
    n, own_ref, grad_ref, momentum_ref, out_ref, blended_ref, local_sem, send_sem, recv_sem
):
    me = lax.axis_index("fsdp")
    place = ring_place(me, n)
    greet([{"fsdp": ring_index(place + 1, n)}, {"fsdp": ring_index(place - 1, n)}])
    local = pltpu.make_async_copy(own_ref, out_ref.at[me], local_sem)
    local.start()
    share = grad_ref.shape[0] // (n // 2)
    tall = piece_of(share) if share < 64 else 64
    block = pl.BlockSpec((tall, grad_ref.shape[1]), lambda i: (i, 0))

    def add(grad_tile, momentum_tile, blended_tile):
        blended_tile[...] = (
            momentum_tile[...].astype(jnp.float32) + grad_tile[...].astype(jnp.float32)
        ).astype(jnp.bfloat16)

    blend = pltpu.emit_pipeline(
        add, grid=(share // tall,), in_specs=[block, block], out_specs=[block]
    )

    def on_step(step):
        at = pl.ds(step * share, share)
        blend(grad_ref.at[at], momentum_ref.at[at], blended_ref.at[at])

    gather_steps(n, place, own_ref, out_ref, send_sem, recv_sem, on_step=on_step)
    local.wait()


def blend_and_gather(grad, momentum, rows):
    n = lax.axis_size("fsdp")
    anywhere = pl.BlockSpec(memory_space=pl.ANY)
    return pl.pallas_call(
        functools.partial(blend_gather_kernel, n),
        out_shape=(
            jax.ShapeDtypeStruct((n,) + rows.shape, rows.dtype),
            jax.ShapeDtypeStruct(grad.shape, jnp.bfloat16),
        ),
        in_specs=[anywhere] * 3,
        out_specs=(anywhere, anywhere),
        scratch_shapes=[
            pltpu.SemaphoreType.DMA(()),
            pltpu.SemaphoreType.DMA((2, n // 2, 2)),
            pltpu.SemaphoreType.DMA((2, n // 2, 2)),
        ],
        compiler_params=pltpu.CompilerParams(
            collective_id=0, has_side_effects=True, vmem_limit_bytes=40 * MIB
        ),
        name="blend_and_gather",
    )(rows, grad, momentum)


def sum_gather_kernel(
    n,
    tps,
    part_ref,
    all_ref,
    own_ref,
    squares_ref,
    land,
    acc,
    others,
    sum_send,
    sum_recv,
    send_sem,
    recv_sem,
    sq_send,
    sq_recv,
):
    half = n // 2
    me = lax.axis_index("fsdp")
    col = lax.axis_index("tp")
    place = ring_place(me, n)
    rows, cols = part_ref.shape[1:]
    width = cols // 2
    piece = piece_of(rows)
    targets = (ring_index(place + 1, n), ring_index(place - 1, n))
    peers = [lax.rem(col + d, tps) for d in range(1, tps)]
    greet([{"fsdp": t} for t in targets] + [{"tp": p} for p in peers])

    copies = {}
    for step in range(half):
        for chunk in (0, 1):
            for way in (0, 1):
                if step == 0 and chunk != way:
                    continue
                lanes = pl.ds(chunk * width, width)
                away = half - step
                owner = ring_index(place + away if way == 0 else place - away, n)
                if step == 0 or (step == 1 and chunk != way):
                    source = part_ref.at[owner, :, lanes]
                else:
                    copies[way, step - 1, chunk].wait_recv()

                    @pl.loop(0, rows // piece)
                    def _(i, way=way, step=step, lanes=lanes, owner=owner):
                        at = pl.ds(pl.multiple_of(i * piece, 16), piece)
                        land[way, step - 1, at, lanes] = (
                            land[way, step - 1, at, lanes].astype(jnp.float32)
                            + part_ref[owner, at, lanes].astype(jnp.float32)
                        ).astype(jnp.bfloat16)

                    source = land.at[way, step - 1, :, lanes]
                copy = pltpu.make_async_remote_copy(
                    src_ref=source,
                    dst_ref=land.at[way, step, :, lanes],
                    send_sem=sum_send.at[way, step, chunk],
                    recv_sem=sum_recv.at[way, step, chunk],
                    device_id={"fsdp": targets[way]},
                    device_id_type=MESH,
                )
                copy.start()
                copies[way, step, chunk] = copy

    for chunk in (0, 1):
        lanes = pl.ds(chunk * width, width)
        for way in (0, 1):
            copies[way, half - 1, chunk].wait_recv()

        @pl.loop(0, rows // piece)
        def _(i, lanes=lanes):
            at = pl.ds(pl.multiple_of(i * piece, 16), piece)
            total = (
                part_ref[me, at, lanes].astype(jnp.float32)
                + land[0, half - 1, at, lanes].astype(jnp.float32)
                + land[1, half - 1, at, lanes].astype(jnp.float32)
            )
            own_ref[at, lanes] = total
            all_ref[me, at, lanes] = total.astype(jnp.bfloat16)

    acc[...] = jnp.zeros_like(acc)

    def on_block(owner, chunk):
        lanes = pl.ds(chunk * width, width)

        @pl.loop(0, rows // piece)
        def _(i):
            at = pl.ds(pl.multiple_of(i * piece, 16), piece)
            block = all_ref[owner, at, lanes].astype(jnp.float32)
            acc[:, lanes] += jnp.sum((block * block).reshape(piece // 8, 8, width), axis=0)

    gather_steps(n, place, all_ref.at[me], all_ref, send_sem, recv_sem, on_block)

    sends = []
    for d, peer in enumerate(peers):
        copy = pltpu.make_async_remote_copy(
            src_ref=acc,
            dst_ref=others.at[d],
            send_sem=sq_send.at[d],
            recv_sem=sq_recv.at[d],
            device_id={"tp": peer},
            device_id_type=MESH,
        )
        copy.start()
        sends.append(copy)
    for copy in copies.values():
        copy.wait_send()
    total = acc[...]
    for d, copy in enumerate(sends):
        copy.wait_recv()
        total = total + others[d]
    squares_ref[...] = jnp.sum(total, axis=0, keepdims=True)
    for copy in sends:
        copy.wait_send()


def sum_and_gather(parts):
    n, rows, cols = parts.shape
    half = n // 2
    tps = lax.axis_size("tp")
    vmem = pl.BlockSpec(memory_space=pltpu.VMEM)
    return pl.pallas_call(
        functools.partial(sum_gather_kernel, n, tps),
        out_shape=(
            jax.ShapeDtypeStruct((n, rows, cols), jnp.bfloat16),
            jax.ShapeDtypeStruct((rows, cols), jnp.float32),
            jax.ShapeDtypeStruct((1, cols), jnp.float32),
        ),
        in_specs=[vmem],
        out_specs=(vmem, vmem, vmem),
        scratch_shapes=[
            pltpu.VMEM((2, half, rows, cols), jnp.bfloat16),
            pltpu.VMEM((8, cols), jnp.float32),
            pltpu.VMEM((tps - 1, 8, cols), jnp.float32),
            pltpu.SemaphoreType.DMA((2, half, 2)),
            pltpu.SemaphoreType.DMA((2, half, 2)),
            pltpu.SemaphoreType.DMA((2, half, 2)),
            pltpu.SemaphoreType.DMA((2, half, 2)),
            pltpu.SemaphoreType.DMA((tps - 1,)),
            pltpu.SemaphoreType.DMA((tps - 1,)),
        ],
        compiler_params=pltpu.CompilerParams(
            collective_id=1, has_side_effects=True, vmem_limit_bytes=48 * MIB
        ),
        name="sum_and_gather",
    )(parts)


def partner(index, bit):
    return index + bit - 2 * bit * lax.rem(lax.div(index, bit), 2)


def bits_below(count):
    return [1 << k for k in range(count.bit_length() - 1)]


def project_gram_kernel(n, tps, part_ref, proj_ref, gram_ref, sums, land, halves, terms, send, recv):
    col = lax.axis_index("tp")
    row = lax.axis_index("fsdp")
    tp_bits, row_bits = bits_below(tps), bits_below(n)
    greet(
        [{"tp": partner(col, b)} for b in tp_bits] + [{"fsdp": partner(row, b)} for b in row_bits]
    )
    used = []

    def exchange(source, target, device):
        k = len(used)
        copy = pltpu.make_async_remote_copy(
            src_ref=source,
            dst_ref=target,
            send_sem=send.at[k],
            recv_sem=recv.at[k],
            device_id=device,
            device_id_type=MESH,
        )
        copy.start()
        used.append(copy)
        copy.wait_recv()

    rows, cols = part_ref.shape
    source, extent, base, top = part_ref, rows, 0, 0
    for k, bit in enumerate(tp_bits):
        extent //= 2
        high = lax.rem(lax.div(col, bit), 2)
        keep = pl.ds(pl.multiple_of(high * extent, 8), extent)
        give = pl.ds(pl.multiple_of((1 - high) * extent, 8), extent)
        exchange(source.at[give], land.at[pl.ds(top, extent)], {"tp": partner(col, bit)})
        base = base + high * extent
        arrived = land[pl.ds(top, extent)]
        if k == len(tp_bits) - 1:
            proj_ref[pl.ds(pl.multiple_of(base, 8), extent)] = source[keep] + arrived
        else:
            sums[pl.ds(top, extent)] = source[keep] + arrived
            source = sums.at[pl.ds(top, extent)]
        top += extent

    def spread(ref, extent):
        for bit in reversed(tp_bits):
            start = 0
            for k, other in enumerate(tp_bits):
                if other < bit or other == bit:
                    start = start + lax.rem(lax.div(col, other), 2) * (ref.shape[0] >> (k + 1))
            held = pl.ds(pl.multiple_of(start, 8), extent)
            exchange(ref.at[held], ref.at[held], {"tp": partner(col, bit)})
            extent *= 2

    spread(proj_ref, extent)

    strip = cols // tps
    first = 0
    for k, bit in enumerate(tp_bits):
        first = first + lax.rem(lax.div(col, bit), 2) * (cols >> (k + 1))
    own = pl.ds(pl.multiple_of(first, strip), strip)
    halves[0] = lax.dot_general(
        proj_ref[:, own],
        proj_ref[...],
        (((0,), (0,)), ((), ())),
        precision=lax.Precision.HIGHEST,
        preferred_element_type=jnp.float32,
    )
    for k, bit in enumerate(row_bits):
        exchange(halves.at[k], terms.at[k], {"fsdp": partner(row, bit)})
        total = halves[k] + terms[k]
        if k == len(row_bits) - 1:
            gram_ref[own] = total
        else:
            halves[k + 1] = total
    spread(gram_ref, strip)
    for copy in used:
        copy.wait_send()


def project_gram(partial_proj):
    rows, cols = partial_proj.shape
    n, tps = lax.axis_size("fsdp"), lax.axis_size("tp")
    stages = 2 * len(bits_below(tps)) + len(bits_below(n)) + len(bits_below(tps))
    levels = len(bits_below(n))
    vmem = pl.BlockSpec(memory_space=pltpu.VMEM)
    return pl.pallas_call(
        functools.partial(project_gram_kernel, n, tps),
        out_shape=(
            jax.ShapeDtypeStruct((rows, cols), jnp.float32),
            jax.ShapeDtypeStruct((cols, cols), jnp.float32),
        ),
        in_specs=[vmem],
        out_specs=(vmem, vmem),
        scratch_shapes=[
            pltpu.VMEM((rows, cols), jnp.float32),
            pltpu.VMEM((rows, cols), jnp.float32),
            pltpu.VMEM((levels, cols // tps, cols), jnp.float32),
            pltpu.VMEM((levels, cols // tps, cols), jnp.float32),
            pltpu.SemaphoreType.DMA((stages,)),
            pltpu.SemaphoreType.DMA((stages,)),
        ],
        compiler_params=pltpu.CompilerParams(
            collective_id=2, has_side_effects=True, vmem_limit_bytes=40 * MIB
        ),
        name="project_gram",
    )(partial_proj)


def per_device(grad, momentum, q_prev):
    rows_dev, cols_dev = grad.shape
    part_rows, width = q_prev.shape
    shards = lax.axis_size("fsdp")
    cols_total = cols_dev * lax.axis_size("tp")
    rows_total = rows_dev * shards
    basis, blended = blend_and_gather(grad, momentum, q_prev)
    basis = basis.reshape(cols_dev, width)
    partial_proj = jnp.dot(blended, basis, preferred_element_type=jnp.float32)
    projected, gram_matrix = project_gram(partial_proj)
    orthonormal = orthonormalize(gram_matrix, projected)
    ortho_low = orthonormal.astype(jnp.bfloat16)
    update_scale = math.sqrt(rows_total / width)
    parts = contract_rows(blended, ortho_low).astype(jnp.bfloat16)
    gathered, reduced, squares = sum_and_gather(parts.reshape(shards, part_rows, width))
    inverse = math.sqrt(cols_total) / (jnp.sqrt(squares) + 1e-06)
    q_new = (reduced * inverse).astype(jnp.bfloat16)
    steer_left = (orthonormal * (update_scale * inverse)).astype(jnp.bfloat16)
    gathered = gathered.reshape(cols_dev, width)
    new_momentum = (
        blended.astype(jnp.float32) - 0.05 * contract_cols(ortho_low, gathered)
    ).astype(jnp.bfloat16)
    update = contract_cols(steer_left, gathered).astype(jnp.bfloat16)
    return (new_momentum, update, q_new)


def solution(mesh):
    return jax.shard_map(
        per_device,
        mesh=mesh,
        in_specs=(P("fsdp", "tp"), P("fsdp", "tp"), P(("tp", "fsdp"), None)),
        out_specs=(P("fsdp", "tp"), P("fsdp", "tp"), P(("tp", "fsdp"), None)),
        check_vma=False,
    )
```

```python
import functools
import math

import jax
import jax.numpy as jnp
from jax import lax
from jax.experimental import pallas as pl
from jax.experimental.pallas import tpu as pltpu
from jax.sharding import PartitionSpec as P

MESH = pl.DeviceIdType.MESH
MIB = 1024 * 1024


def contract_rows(left, right, precision=None):
    return lax.dot_general(
        left,
        right,
        (((0,), (0,)), ((), ())),
        precision=precision,
        preferred_element_type=jnp.float32,
    )


def contract_cols(left, right):
    return lax.dot_general(
        left, right, (((1,), (1,)), ((), ())), preferred_element_type=jnp.float32
    )


def factor_inverse(block):
    size = block.shape[0]
    group = 16
    row = lax.broadcasted_iota(jnp.int32, (size, 1), 0)
    eye = (
        lax.broadcasted_iota(jnp.int32, (size, size), 0)
        == lax.broadcasted_iota(jnp.int32, (size, size), 1)
    )

    def eliminate(step, carry):
        left, right = carry
        for s in range(group):
            active = (row > s) & (row < size - group * step)
            column = jnp.broadcast_to(left[:, s : s + 1], left.shape)
            inverse = 1.0 / column[s : s + 1, :]
            column = jnp.where(active, column, 0.0)
            left, right = (
                left - column * (left[s : s + 1, :] * inverse),
                right - column * (right[s : s + 1, :] * inverse),
            )
        left = pltpu.roll(jnp.concatenate([left[group:], left[:group]], axis=0), size - group, 1)
        right = jnp.concatenate([right[group:], right[:group]], axis=0)
        return left, right

    left, right = lax.fori_loop(
        0, size // group, eliminate, (block, jnp.where(eye, 1.0, 0.0).astype(jnp.float32))
    )
    diagonal = jnp.sum(jnp.where(eye, left, 0.0), axis=1, keepdims=True)
    return right / jnp.sqrt(diagonal)


def orthonormalize_kernel(block, gram_ref, proj_ref, ortho_ref, gram, proj):
    size = gram_ref.shape[0]
    gram[...] = gram_ref[...]
    proj[...] = proj_ref[...]

    def times_transposed(left, right):
        return lax.dot_general(
            left,
            right,
            (((1,), (1,)), ((), ())),
            precision=lax.Precision.HIGHEST,
            preferred_element_type=jnp.float32,
        )

    for start in range(0, size, block):
        end = start + block
        inverse = factor_inverse(gram[start:end, start:end])
        solved = times_transposed(proj[:, start:end], inverse)
        ortho_ref[:, start:end] = solved
        if end < size:
            panel = times_transposed(gram[end:, start:end], inverse)
            gram[end:, end:] -= times_transposed(panel, panel)
            proj[:, end:] -= times_transposed(solved, panel)


def orthonormalize(gram_matrix, projected):
    vmem = pl.BlockSpec(memory_space=pltpu.VMEM)
    return pl.pallas_call(
        functools.partial(orthonormalize_kernel, 128),
        out_shape=jax.ShapeDtypeStruct(projected.shape, jnp.float32),
        in_specs=[vmem, vmem],
        out_specs=vmem,
        scratch_shapes=[
            pltpu.VMEM(gram_matrix.shape, jnp.float32),
            pltpu.VMEM(projected.shape, jnp.float32),
        ],
        compiler_params=pltpu.CompilerParams(vmem_limit_bytes=40 * MIB),
        name="orthonormalize",
    )(gram_matrix, projected)


def ring_place(index, n):
    pair = lax.div(index, 2)
    return pair + lax.rem(index, 2) * (n - 1 - 2 * pair)


def ring_index(place, n):
    place = lax.rem(place + 2 * n, n)
    upper = lax.div(place, n // 2)
    return 2 * place + upper * (2 * n - 1 - 4 * place)


def piece_of(rows):
    return max(p for p in range(16, 209, 16) if rows % p == 0)


def greet(devices):
    barrier = pltpu.get_barrier_semaphore()
    for device in devices:
        pl.semaphore_signal(barrier, inc=1, device_id=device, device_id_type=MESH)
    pl.semaphore_wait(barrier, len(devices))


def gather_steps(n, place, own_ref, out_ref, send_sem, recv_sem, on_block=None, on_step=None):
    half = n // 2
    width = out_ref.shape[2] // 2
    targets = (ring_index(place + 1, n), ring_index(place - 1, n))
    copies = {}
    for step in range(half):
        for chunk in (0, 1):
            for way in (0, 1):
                if step == half - 1 and chunk != way:
                    continue
                owner = ring_index(place - step if way == 0 else place + step, n)
                lanes = pl.ds(chunk * width, width)
                if step > 0:
                    copies[way, step - 1, chunk].wait_recv()
                source = own_ref if step == 0 else out_ref.at[owner]
                copy = pltpu.make_async_remote_copy(
                    src_ref=source.at[:, lanes],
                    dst_ref=out_ref.at[owner, :, lanes],
                    send_sem=send_sem.at[way, step, chunk],
                    recv_sem=recv_sem.at[way, step, chunk],
                    device_id={"fsdp": targets[way]},
                    device_id_type=MESH,
                )
                copy.start()
                copies[way, step, chunk] = copy
                if on_block is not None and (step > 0 or way == 0):
                    on_block(owner, chunk)
        if on_step is not None:
            on_step(step)
    for way in (0, 1):
        copies[way, half - 2, 1 - way].wait_recv()
        if on_block is not None:
            owner = ring_index(place - half + 1 if way == 0 else place + half - 1, n)
            on_block(owner, 1 - way)
    for way in (0, 1):
        copies[way, half - 1, way].wait_recv()
        if on_block is not None:
            on_block(ring_index(place + half, n), way)
    for copy in copies.values():
        copy.wait_send()


def blend_gather_kernel(
    n, own_ref, grad_ref, momentum_ref, out_ref, blended_ref, local_sem, send_sem, recv_sem
):
    me = lax.axis_index("fsdp")
    place = ring_place(me, n)
    greet([{"fsdp": ring_index(place + 1, n)}, {"fsdp": ring_index(place - 1, n)}])
    local = pltpu.make_async_copy(own_ref, out_ref.at[me], local_sem)
    local.start()
    share = grad_ref.shape[0] // (n // 2)
    tall = piece_of(share) if share < 64 else 64
    block = pl.BlockSpec((tall, grad_ref.shape[1]), lambda i: (i, 0))

    def add(grad_tile, momentum_tile, blended_tile):
        blended_tile[...] = (
            momentum_tile[...].astype(jnp.float32) + grad_tile[...].astype(jnp.float32)
        ).astype(jnp.bfloat16)

    blend = pltpu.emit_pipeline(
        add, grid=(share // tall,), in_specs=[block, block], out_specs=[block]
    )

    def on_step(step):
        at = pl.ds(step * share, share)
        blend(grad_ref.at[at], momentum_ref.at[at], blended_ref.at[at])

    gather_steps(n, place, own_ref, out_ref, send_sem, recv_sem, on_step=on_step)
    local.wait()


def blend_and_gather(grad, momentum, rows):
    n = lax.axis_size("fsdp")
    anywhere = pl.BlockSpec(memory_space=pl.ANY)
    return pl.pallas_call(
        functools.partial(blend_gather_kernel, n),
        out_shape=(
            jax.ShapeDtypeStruct((n,) + rows.shape, rows.dtype),
            jax.ShapeDtypeStruct(grad.shape, jnp.bfloat16),
        ),
        in_specs=[anywhere] * 3,
        out_specs=(anywhere, anywhere),
        scratch_shapes=[
            pltpu.SemaphoreType.DMA(()),
            pltpu.SemaphoreType.DMA((2, n // 2, 2)),
            pltpu.SemaphoreType.DMA((2, n // 2, 2)),
        ],
        compiler_params=pltpu.CompilerParams(
            collective_id=0, has_side_effects=True, vmem_limit_bytes=40 * MIB
        ),
        name="blend_and_gather",
    )(rows, grad, momentum)


def sum_gather_kernel(
    n,
    tps,
    part_ref,
    all_ref,
    own_ref,
    squares_ref,
    land,
    acc,
    others,
    sum_send,
    sum_recv,
    send_sem,
    recv_sem,
    sq_send,
    sq_recv,
):
    half = n // 2
    me = lax.axis_index("fsdp")
    col = lax.axis_index("tp")
    place = ring_place(me, n)
    rows, cols = part_ref.shape[1:]
    width = cols // 2
    piece = piece_of(rows)
    targets = (ring_index(place + 1, n), ring_index(place - 1, n))
    peers = [lax.rem(col + d, tps) for d in range(1, tps)]
    greet([{"fsdp": t} for t in targets] + [{"tp": p} for p in peers])

    copies = {}
    for step in range(half):
        for chunk in (0, 1):
            for way in (0, 1):
                if step == 0 and chunk != way:
                    continue
                lanes = pl.ds(chunk * width, width)
                away = half - step
                owner = ring_index(place + away if way == 0 else place - away, n)
                if step == 0 or (step == 1 and chunk != way):
                    source = part_ref.at[owner, :, lanes]
                else:
                    copies[way, step - 1, chunk].wait_recv()

                    @pl.loop(0, rows // piece)
                    def _(i, way=way, step=step, lanes=lanes, owner=owner):
                        at = pl.ds(pl.multiple_of(i * piece, 16), piece)
                        land[way, step - 1, at, lanes] = (
                            land[way, step - 1, at, lanes].astype(jnp.float32)
                            + part_ref[owner, at, lanes].astype(jnp.float32)
                        ).astype(jnp.bfloat16)

                    source = land.at[way, step - 1, :, lanes]
                copy = pltpu.make_async_remote_copy(
                    src_ref=source,
                    dst_ref=land.at[way, step, :, lanes],
                    send_sem=sum_send.at[way, step, chunk],
                    recv_sem=sum_recv.at[way, step, chunk],
                    device_id={"fsdp": targets[way]},
                    device_id_type=MESH,
                )
                copy.start()
                copies[way, step, chunk] = copy

    for chunk in (0, 1):
        lanes = pl.ds(chunk * width, width)
        for way in (0, 1):
            copies[way, half - 1, chunk].wait_recv()

        @pl.loop(0, rows // piece)
        def _(i, lanes=lanes):
            at = pl.ds(pl.multiple_of(i * piece, 16), piece)
            total = (
                part_ref[me, at, lanes].astype(jnp.float32)
                + land[0, half - 1, at, lanes].astype(jnp.float32)
                + land[1, half - 1, at, lanes].astype(jnp.float32)
            )
            own_ref[at, lanes] = total
            all_ref[me, at, lanes] = total.astype(jnp.bfloat16)

    acc[...] = jnp.zeros_like(acc)

    def on_block(owner, chunk):
        lanes = pl.ds(chunk * width, width)

        @pl.loop(0, rows // piece)
        def _(i):
            at = pl.ds(pl.multiple_of(i * piece, 16), piece)
            block = all_ref[owner, at, lanes].astype(jnp.float32)
            acc[:, lanes] += jnp.sum((block * block).reshape(piece // 8, 8, width), axis=0)

    gather_steps(n, place, all_ref.at[me], all_ref, send_sem, recv_sem, on_block)

    sends = []
    for d, peer in enumerate(peers):
        copy = pltpu.make_async_remote_copy(
            src_ref=acc,
            dst_ref=others.at[d],
            send_sem=sq_send.at[d],
            recv_sem=sq_recv.at[d],
            device_id={"tp": peer},
            device_id_type=MESH,
        )
        copy.start()
        sends.append(copy)
    for copy in copies.values():
        copy.wait_send()
    total = acc[...]
    for d, copy in enumerate(sends):
        copy.wait_recv()
        total = total + others[d]
    squares_ref[...] = jnp.sum(total, axis=0, keepdims=True)
    for copy in sends:
        copy.wait_send()


def sum_and_gather(parts):
    n, rows, cols = parts.shape
    half = n // 2
    tps = lax.axis_size("tp")
    vmem = pl.BlockSpec(memory_space=pltpu.VMEM)
    return pl.pallas_call(
        functools.partial(sum_gather_kernel, n, tps),
        out_shape=(
            jax.ShapeDtypeStruct((n, rows, cols), jnp.bfloat16),
            jax.ShapeDtypeStruct((rows, cols), jnp.float32),
            jax.ShapeDtypeStruct((1, cols), jnp.float32),
        ),
        in_specs=[vmem],
        out_specs=(vmem, vmem, vmem),
        scratch_shapes=[
            pltpu.VMEM((2, half, rows, cols), jnp.bfloat16),
            pltpu.VMEM((8, cols), jnp.float32),
            pltpu.VMEM((tps - 1, 8, cols), jnp.float32),
            pltpu.SemaphoreType.DMA((2, half, 2)),
            pltpu.SemaphoreType.DMA((2, half, 2)),
            pltpu.SemaphoreType.DMA((2, half, 2)),
            pltpu.SemaphoreType.DMA((2, half, 2)),
            pltpu.SemaphoreType.DMA((tps - 1,)),
            pltpu.SemaphoreType.DMA((tps - 1,)),
        ],
        compiler_params=pltpu.CompilerParams(
            collective_id=1, has_side_effects=True, vmem_limit_bytes=48 * MIB
        ),
        name="sum_and_gather",
    )(parts)


def partner(index, bit):
    return index + bit - 2 * bit * lax.rem(lax.div(index, bit), 2)


def bits_below(count):
    return [1 << k for k in range(count.bit_length() - 1)]


def project_gram_kernel(n, tps, part_ref, proj_ref, gram_ref, sums, land, halves, terms, send, recv):
    col = lax.axis_index("tp")
    row = lax.axis_index("fsdp")
    tp_bits, row_bits = bits_below(tps), bits_below(n)
    greet(
        [{"tp": partner(col, b)} for b in tp_bits] + [{"fsdp": partner(row, b)} for b in row_bits]
    )
    used = []

    def exchange(source, target, device):
        k = len(used)
        copy = pltpu.make_async_remote_copy(
            src_ref=source,
            dst_ref=target,
            send_sem=send.at[k],
            recv_sem=recv.at[k],
            device_id=device,
            device_id_type=MESH,
        )
        copy.start()
        used.append(copy)
        copy.wait_recv()

    rows, cols = part_ref.shape
    source, extent, base, top = part_ref, rows, 0, 0
    for k, bit in enumerate(tp_bits):
        extent //= 2
        high = lax.rem(lax.div(col, bit), 2)
        keep = pl.ds(pl.multiple_of(high * extent, 8), extent)
        give = pl.ds(pl.multiple_of((1 - high) * extent, 8), extent)
        exchange(source.at[give], land.at[pl.ds(top, extent)], {"tp": partner(col, bit)})
        base = base + high * extent
        arrived = land[pl.ds(top, extent)]
        if k == len(tp_bits) - 1:
            proj_ref[pl.ds(pl.multiple_of(base, 8), extent)] = source[keep] + arrived
        else:
            sums[pl.ds(top, extent)] = source[keep] + arrived
            source = sums.at[pl.ds(top, extent)]
        top += extent

    def spread(ref, extent):
        for bit in reversed(tp_bits):
            start = 0
            for k, other in enumerate(tp_bits):
                if other < bit or other == bit:
                    start = start + lax.rem(lax.div(col, other), 2) * (ref.shape[0] >> (k + 1))
            held = pl.ds(pl.multiple_of(start, 8), extent)
            exchange(ref.at[held], ref.at[held], {"tp": partner(col, bit)})
            extent *= 2

    spread(proj_ref, extent)

    strip = cols // tps
    first = 0
    for k, bit in enumerate(tp_bits):
        first = first + lax.rem(lax.div(col, bit), 2) * (cols >> (k + 1))
    own = pl.ds(pl.multiple_of(first, strip), strip)
    halves[0] = lax.dot_general(
        proj_ref[:, own],
        proj_ref[...],
        (((0,), (0,)), ((), ())),
        precision=lax.Precision.HIGHEST,
        preferred_element_type=jnp.float32,
    )
    part = strip // 2
    high = lax.rem(row, 2)
    keep = pl.ds(pl.multiple_of(high * part, 8), part)
    give = pl.ds(pl.multiple_of((1 - high) * part, 8), part)
    mine = pl.ds(pl.multiple_of(first + high * part, 8), part)
    low = pl.ds(0, part)
    exchange(halves.at[0, give], terms.at[0, low], {"fsdp": partner(row, 1)})
    total = halves[0, keep] + terms[0, low]
    for k, bit in enumerate(row_bits[1:], 1):
        halves[k, low] = total
        exchange(halves.at[k, low], terms.at[k, low], {"fsdp": partner(row, bit)})
        total = halves[k, low] + terms[k, low]
    gram_ref[mine] = total
    exchange(gram_ref.at[mine], gram_ref.at[mine], {"fsdp": partner(row, 1)})
    spread(gram_ref, strip)
    for copy in used:
        copy.wait_send()


def project_gram(partial_proj):
    rows, cols = partial_proj.shape
    n, tps = lax.axis_size("fsdp"), lax.axis_size("tp")
    stages = 2 * len(bits_below(tps)) + len(bits_below(n)) + 1 + len(bits_below(tps))
    levels = len(bits_below(n))
    vmem = pl.BlockSpec(memory_space=pltpu.VMEM)
    return pl.pallas_call(
        functools.partial(project_gram_kernel, n, tps),
        out_shape=(
            jax.ShapeDtypeStruct((rows, cols), jnp.float32),
            jax.ShapeDtypeStruct((cols, cols), jnp.float32),
        ),
        in_specs=[vmem],
        out_specs=(vmem, vmem),
        scratch_shapes=[
            pltpu.VMEM((rows, cols), jnp.float32),
            pltpu.VMEM((rows, cols), jnp.float32),
            pltpu.VMEM((levels, cols // tps, cols), jnp.float32),
            pltpu.VMEM((levels, cols // tps, cols), jnp.float32),
            pltpu.SemaphoreType.DMA((stages,)),
            pltpu.SemaphoreType.DMA((stages,)),
        ],
        compiler_params=pltpu.CompilerParams(
            collective_id=2, has_side_effects=True, vmem_limit_bytes=40 * MIB
        ),
        name="project_gram",
    )(partial_proj)


def per_device(grad, momentum, q_prev):
    rows_dev, cols_dev = grad.shape
    part_rows, width = q_prev.shape
    shards = lax.axis_size("fsdp")
    cols_total = cols_dev * lax.axis_size("tp")
    rows_total = rows_dev * shards
    basis, blended = blend_and_gather(grad, momentum, q_prev)
    basis = basis.reshape(cols_dev, width)
    partial_proj = jnp.dot(blended, basis, preferred_element_type=jnp.float32)
    projected, gram_matrix = project_gram(partial_proj)
    orthonormal = orthonormalize(gram_matrix, projected)
    ortho_low = orthonormal.astype(jnp.bfloat16)
    update_scale = math.sqrt(rows_total / width)
    parts = contract_rows(blended, ortho_low).astype(jnp.bfloat16)
    gathered, reduced, squares = sum_and_gather(parts.reshape(shards, part_rows, width))
    inverse = math.sqrt(cols_total) / (jnp.sqrt(squares) + 1e-06)
    q_new = (reduced * inverse).astype(jnp.bfloat16)
    steer_left = (orthonormal * (update_scale * inverse)).astype(jnp.bfloat16)
    gathered = gathered.reshape(cols_dev, width)
    new_momentum = (
        blended.astype(jnp.float32) - 0.05 * contract_cols(ortho_low, gathered)
    ).astype(jnp.bfloat16)
    update = contract_cols(steer_left, gathered).astype(jnp.bfloat16)
    return (new_momentum, update, q_new)


def solution(mesh):
    return jax.shard_map(
        per_device,
        mesh=mesh,
        in_specs=(P("fsdp", "tp"), P("fsdp", "tp"), P(("tp", "fsdp"), None)),
        out_specs=(P("fsdp", "tp"), P("fsdp", "tp"), P(("tp", "fsdp"), None)),
        check_vma=False,
    )
```
